32 devices in a mesh: rows: 16 (over z, y, x), cent: 2 (over core).
Axes of the slice: x: 2, y: 2, z: 4, core: 2. Of those that a mesh axis runs over, the one named last changes fastest.
Arguments:
- passages: bfloat16 [65536, 768], P('rows'), may hold values from -8 to 8
- centroids: bfloat16 [8192, 768], P('cent'), may hold values from -8 to 8
Outputs:
- new_centroids: float32 [8192, 768], P('cent')
- log_row_scale: float32 [65536], P('rows')
The draws below stay inside these ranges and needn't reach their ends.
All inputs are finite; a program needn't handle non-finite values.
Results may differ from the reference program's by a relative error of at most 0.0042.
Values sent between devices are 32-bit elements; how exact they have to be, the bound alone decides.
A program may use at most 192 MiB of HBM per device.

```python
import jax
import jax.numpy as jnp
from jax import lax

D = 768
K = 8192
ROWS_DEV = 4096
ITERS = 3
ROWS = 65536
N_ROWS = 16


def shared_directions(key):
    inner = jax.random.fold_in(key, 101)
    return jnp.clip(jax.random.normal(inner, (K, D), jnp.float32), -6.0, 6.0)


def draw_centroids(key, part):
    directions = shared_directions(key)
    result = directions
    return jnp.clip(result, -8.0, 8.0).astype(jnp.bfloat16)


def draw_passages(key, part):
    directions = shared_directions(key)
    inner = jax.random.fold_in(key, 202)
    first_key, second_key, third_key, order_key, mix_key, noise_key = jax.random.split(inner, 6)
    first = jax.random.randint(first_key, (ROWS,), 0, K, dtype=jnp.int32)
    second = jax.random.randint(second_key, (ROWS,), 0, K, dtype=jnp.int32)
    third = jax.random.randint(third_key, (ROWS,), 0, K, dtype=jnp.int32)
    skewed = first * second // K * third // K
    order = jax.random.permutation(order_key, K)
    cluster = jnp.take(order, skewed)
    own = jnp.take(directions, cluster, axis=0)
    closeness = jax.random.uniform(mix_key, (ROWS, 1), jnp.float32, 0.3, 0.8)
    noise = jnp.clip(jax.random.normal(noise_key, (ROWS, D), jnp.float32), -4.0, 4.0)
    result = closeness * own + jnp.sqrt(1.0 - closeness * closeness) * noise
    return jnp.clip(result, -8.0, 8.0).astype(jnp.bfloat16)


def setup_inputs(seed: int = 0) -> dict:
    streams_of = jax.random.split(jax.random.key(seed), 3)
    return {
        "passages": draw_passages(jax.random.fold_in(streams_of[2], 71), 0),
        "centroids": draw_centroids(jax.random.fold_in(streams_of[2], 71), 0),
    }


def unit_scale(values):
    full = values.astype(jnp.float32)
    return full * lax.rsqrt(lax.optimization_barrier(jnp.mean(full * full, axis=-1, keepdims=True)) + 1e-06)

def reference(passages, centroids):
    unit_rows = unit_scale(passages).astype(jnp.bfloat16)
    unit_cents = unit_scale(centroids).astype(jnp.bfloat16)
    blocks = unit_rows.reshape(N_ROWS, ROWS_DEV, D)

    def block_kernel(block):
        cosine = jnp.dot(block, unit_cents.T, preferred_element_type=jnp.float32) / D
        return jnp.exp((cosine - 1.0) / 0.05)
    kernel = lax.map(block_kernel, blocks).reshape(ROWS, K)
    ratio = jnp.float32(ROWS) / jnp.float32(K)
    row_scale = jnp.ones((ROWS,), jnp.float32)
    for step in range(ITERS):
        col_total = jnp.dot(row_scale, kernel, precision=lax.Precision.HIGHEST)
        col_scale = ratio / col_total
        row_total = jnp.dot(kernel, col_scale, precision=lax.Precision.HIGHEST)
        row_scale = 1.0 / row_total
    kernel_blocks = kernel.reshape(N_ROWS, ROWS_DEV, K)
    scale_blocks = row_scale.reshape(N_ROWS, ROWS_DEV)

    def accumulate(total, items):
        kernel_block, scale_block, row_block = items
        plan = (scale_block[:, None] * kernel_block).astype(jnp.bfloat16)
        part = lax.dot_general(plan, row_block, (((0,), (0,)), ((), ())), preferred_element_type=jnp.float32)
        return (total + part, None)
    sums, unused = lax.scan(accumulate, jnp.zeros((K, D), jnp.float32), (kernel_blocks, scale_blocks, blocks))
    new_centroids = sums * lax.rsqrt(lax.optimization_barrier(jnp.mean(sums * sums, axis=-1, keepdims=True)) + 1e-06)
    return (new_centroids, jnp.log(row_scale))
```

```python
import functools
import math

import jax
import jax.numpy as jnp
from jax import lax
from jax.experimental import pallas as pl
from jax.experimental.pallas import tpu as pltpu
from jax.sharding import PartitionSpec as P

ITERS = 3
MESH = pl.DeviceIdType.MESH
F32 = jnp.float32
BF16 = jnp.bfloat16
CENT_BLOCK = 256
ROW_BLOCK = 1024
PASS_BLOCK = 512


def unit_scale(values):
    full = values.astype(F32)
    return full * lax.rsqrt(jnp.mean(full * full, axis=-1, keepdims=True) + 1e-06)


def split_rows(vector):
    high = vector.astype(BF16).astype(F32)
    low = vector - high
    which = lax.broadcasted_iota(jnp.int32, (16, vector.shape[1]), 0)
    return jnp.where(which == 0, high, jnp.where(which == 1, low, 0.0)).astype(BF16)


def blocks(size, block, body):
    block = min(size, block)

    def step(index, carry):
        body(pl.ds(pl.multiple_of(index * block, block), block), block, index)
        return carry

    lax.fori_loop(0, size // block, step, 0)


def sinkhorn_kernel(
    n_rows, n_cent, ratio,
    rows_hbm, cents_hbm, sums_hbm, log_ref,
    kern, unit, cents, out_buf, col_vec, row_vec, row_scale,
    col_slots, row_slots, in_sem, out_sem, col_send, col_recv, row_send, row_recv,
):
    rows, width = unit.shape
    n_local = cents.shape[0]
    me_row = lax.axis_index("rows")
    me_cent = lax.axis_index("cent")
    part = rows // 4
    loads = [
        pltpu.make_async_copy(
            rows_hbm.at[pl.ds(q * part, part)], unit.at[pl.ds(q * part, part)], in_sem.at[q]
        )
        for q in range(4)
    ]
    loads.append(pltpu.make_async_copy(cents_hbm, cents, in_sem.at[4]))
    for load in loads:
        load.start()

    barrier = pltpu.get_barrier_semaphore()
    for off in range(1, n_rows):
        pl.semaphore_signal(
            barrier, inc=1, device_id={"rows": lax.rem(me_row + off, n_rows)}, device_id_type=MESH
        )
    for off in range(1, n_cent):
        pl.semaphore_signal(
            barrier, inc=1, device_id={"cent": lax.rem(me_cent + off, n_cent)}, device_id_type=MESH
        )

    for q in range(4):
        loads[q].wait()

        def normalize(where, block, index, q=q):
            at = pl.ds(pl.multiple_of(q * part + index * block, block), block)
            unit[at, :] = unit_scale(unit[at, :]).astype(BF16)

        blocks(part, 256, normalize)
    loads[4].wait()

    slope = 20.0 * math.log2(math.e) / width
    offset = 20.0 * math.log2(math.e)
    row_block = min(rows, ROW_BLOCK)

    def make_kernel(where, block, index):
        unit_cents = unit_scale(cents[where, :]).astype(BF16)
        acc = jnp.zeros((block, 128), F32)
        for b in range(rows // row_block):
            here = slice(b * row_block, (b + 1) * row_block)
            dot = lax.dot_general(
                unit_cents, unit[here, :], (((1,), (1,)), ((), ())), preferred_element_type=F32
            )
            value = jnp.exp2(dot * slope - offset)
            kern[where, here] = value.astype(BF16)
            for lane in range(row_block // 128):
                acc = acc + value[:, lane * 128:(lane + 1) * 128]
        col_slots[0, 0, :, where] = jnp.sum(acc.T, axis=0, keepdims=True)

    blocks(n_local, CENT_BLOCK, make_kernel)
    pl.semaphore_wait(barrier, n_rows - 1 + n_cent - 1)

    for t in range(ITERS):
        copies = []
        for off in range(1, n_rows):
            copies.append(pltpu.make_async_remote_copy(
                src_ref=col_slots.at[t, 0],
                dst_ref=col_slots.at[t, off],
                send_sem=col_send.at[t, off],
                recv_sem=col_recv.at[t, off],
                device_id={"rows": lax.rem(me_row + off, n_rows)},
                device_id_type=MESH,
            ))
        for copy in copies:
            copy.start()
        for copy in copies:
            copy.wait()
        total = col_slots[t, 0]
        for off in range(1, n_rows):
            total = total + col_slots[t, off]
        col_vec[...] = split_rows(ratio / total)

        def row_pass(where, block, index):
            mass = jnp.dot(col_vec[...], kern[:, where], preferred_element_type=F32)
            row_slots[t, me_cent, :, where] = jnp.sum(mass, axis=0, keepdims=True)

        blocks(rows, PASS_BLOCK, row_pass)
        copies = []
        for off in range(1, n_cent):
            copies.append(pltpu.make_async_remote_copy(
                src_ref=row_slots.at[t, me_cent],
                dst_ref=row_slots.at[t, me_cent],
                send_sem=row_send.at[t, off],
                recv_sem=row_recv.at[t, off],
                device_id={"cent": lax.rem(me_cent + off, n_cent)},
                device_id_type=MESH,
            ))
        for copy in copies:
            copy.start()
        for copy in copies:
            copy.wait()
        total = row_slots[t, 0]
        for other in range(1, n_cent):
            total = total + row_slots[t, other]
        scale = 1.0 / total
        if t < ITERS - 1:
            row_vec[...] = split_rows(scale)

            def col_pass(where, block, index):
                mass = lax.dot_general(
                    row_vec[...], kern[where, :], (((1,), (1,)), ((), ())),
                    preferred_element_type=F32,
                )
                col_slots[t + 1, 0, :, where] = jnp.sum(mass, axis=0, keepdims=True)

            blocks(n_local, PASS_BLOCK, col_pass)
        else:
            row_scale[...] = scale
            log_ref[...] = jnp.log(scale)

    out_block = min(CENT_BLOCK, n_local)
    steps = n_local // out_block

    def store(index, slot):
        at = pl.ds(pl.multiple_of(index * out_block, out_block), out_block)
        return pltpu.make_async_copy(out_buf.at[slot], sums_hbm.at[at], out_sem.at[slot])

    def weigh(index, carry):
        slot = lax.rem(index, 2)
        at = pl.ds(pl.multiple_of(index * out_block, out_block), out_block)

        @pl.when(index >= 2)
        def _():
            store(index - 2, slot).wait()

        total = jnp.zeros((out_block, width), F32)
        for b in range(rows // row_block):
            here = slice(b * row_block, (b + 1) * row_block)
            plan = (kern[at, here].astype(F32) * row_scale[:, here]).astype(BF16)
            total = total + jnp.dot(plan, unit[here, :], preferred_element_type=F32)
        out_buf[slot] = total
        store(index, slot).start()
        return carry

    lax.fori_loop(0, steps, weigh, 0)
    for index in range(max(steps - 2, 0), steps):
        store(index, index % 2).wait()


def balance(passages, centroids, n_rows, n_cent):
    rows, width = passages.shape
    n_local = centroids.shape[0]
    ratio = float(rows * n_rows) / float(n_local * n_cent)
    dma = pltpu.SemaphoreType.DMA
    return pl.pallas_call(
        functools.partial(sinkhorn_kernel, n_rows, n_cent, ratio),
        out_shape=(
            jax.ShapeDtypeStruct((n_local, width), F32),
            jax.ShapeDtypeStruct((1, rows), F32),
        ),
        in_specs=[pl.BlockSpec(memory_space=pl.ANY)] * 2,
        out_specs=(pl.BlockSpec(memory_space=pl.ANY), pl.BlockSpec(memory_space=pltpu.VMEM)),
        scratch_shapes=[
            pltpu.VMEM((n_local, rows), BF16),
            pltpu.VMEM((rows, width), BF16),
            pltpu.VMEM((n_local, width), BF16),
            pltpu.VMEM((2, min(CENT_BLOCK, n_local), width), F32),
            pltpu.VMEM((16, n_local), BF16),
            pltpu.VMEM((16, rows), BF16),
            pltpu.VMEM((1, rows), F32),
            pltpu.VMEM((ITERS, n_rows, 1, n_local), F32),
            pltpu.VMEM((ITERS, n_cent, 1, rows), F32),
            dma((5,)), dma((2,)),
            dma((ITERS, n_rows)), dma((ITERS, n_rows)),
            dma((ITERS, n_cent)), dma((ITERS, n_cent)),
        ],
        compiler_params=pltpu.CompilerParams(
            collective_id=0, has_side_effects=True, vmem_limit_bytes=60 * 1024 * 1024
        ),
        name="balance",
    )(passages, centroids)


def shards(n_rows, n_cent, passages, centroids):
    terms, logs = balance(passages, centroids, n_rows, n_cent)
    sums = lax.psum(terms, "rows")
    new_centroids = sums * lax.rsqrt(jnp.mean(sums * sums, axis=-1, keepdims=True) + 1e-06)
    return (new_centroids, logs.reshape(-1))


def solution(mesh):
    placed = (P("rows", None), P("cent", None))
    return jax.shard_map(
        functools.partial(shards, mesh.shape["rows"], mesh.shape["cent"]),
        mesh=mesh, in_specs=placed, out_specs=(P("cent", None), P("rows")), check_vma=False,
    )
```

```python
import functools
import math

import jax
import jax.numpy as jnp
from jax import lax
from jax.experimental import pallas as pl
from jax.experimental.pallas import tpu as pltpu
from jax.sharding import PartitionSpec as P

ITERS = 3
MESH = pl.DeviceIdType.MESH
F32 = jnp.float32
BF16 = jnp.bfloat16
CENT_BLOCK = 256
ROW_BLOCK = 1024
PASS_BLOCK = 512
PIECES = 4


def unit_scale(values):
    full = values.astype(F32)
    return full * lax.rsqrt(jnp.mean(full * full, axis=-1, keepdims=True) + 1e-06)


def split_rows(vector):
    high = vector.astype(BF16).astype(F32)
    low = vector - high
    which = lax.broadcasted_iota(jnp.int32, (16, vector.shape[1]), 0)
    return jnp.where(which == 0, high, jnp.where(which == 1, low, 0.0)).astype(BF16)


def blocks(size, block, body):
    block = min(size, block)

    def step(index, carry):
        body(pl.ds(pl.multiple_of(index * block, block), block), block, index)
        return carry

    lax.fori_loop(0, size // block, step, 0)


def sinkhorn_kernel(
    n_rows, n_cent, ratio,
    rows_hbm, cents_hbm, sums_hbm, log_ref,
    kern, unit, cents, out_buf, col_vec, row_vec, row_scale,
    col_slots, row_slots, in_sem, out_sem, col_send, col_recv, row_send, row_recv,
):
    rows, width = unit.shape
    n_local = cents.shape[0]
    me_row = lax.axis_index("rows")
    me_cent = lax.axis_index("cent")
    part = rows // 4
    loads = [
        pltpu.make_async_copy(
            rows_hbm.at[pl.ds(q * part, part)], unit.at[pl.ds(q * part, part)], in_sem.at[q]
        )
        for q in range(4)
    ]
    loads.append(pltpu.make_async_copy(cents_hbm, cents, in_sem.at[4]))
    for load in loads:
        load.start()

    barrier = pltpu.get_barrier_semaphore()
    for off in range(1, n_rows):
        pl.semaphore_signal(
            barrier, inc=1, device_id={"rows": lax.rem(me_row + off, n_rows)}, device_id_type=MESH
        )
    for off in range(1, n_cent):
        pl.semaphore_signal(
            barrier, inc=1, device_id={"cent": lax.rem(me_cent + off, n_cent)}, device_id_type=MESH
        )

    for q in range(4):
        loads[q].wait()

        def normalize(where, block, index, q=q):
            at = pl.ds(pl.multiple_of(q * part + index * block, block), block)
            unit[at, :] = unit_scale(unit[at, :]).astype(BF16)

        blocks(part, 256, normalize)
    loads[4].wait()

    slope = 20.0 * math.log2(math.e) / width
    offset = 20.0 * math.log2(math.e)
    row_block = min(rows, ROW_BLOCK)

    def make_kernel(where, block, index):
        unit_cents = unit_scale(cents[where, :]).astype(BF16)
        acc = jnp.zeros((block, 128), F32)
        for b in range(rows // row_block):
            here = slice(b * row_block, (b + 1) * row_block)
            dot = lax.dot_general(
                unit_cents, unit[here, :], (((1,), (1,)), ((), ())), preferred_element_type=F32
            )
            value = jnp.exp2(dot * slope - offset)
            kern[where, here] = value.astype(BF16)
            for lane in range(row_block // 128):
                acc = acc + value[:, lane * 128:(lane + 1) * 128]
        col_slots[0, 0, :, where] = jnp.sum(acc.T, axis=0, keepdims=True)

    blocks(n_local, CENT_BLOCK, make_kernel)
    pl.semaphore_wait(barrier, n_rows - 1 + n_cent - 1)

    for t in range(ITERS):
        copies = []
        for off in range(1, n_rows):
            copies.append(pltpu.make_async_remote_copy(
                src_ref=col_slots.at[t, 0],
                dst_ref=col_slots.at[t, off],
                send_sem=col_send.at[t, off],
                recv_sem=col_recv.at[t, off],
                device_id={"rows": lax.rem(me_row + off, n_rows)},
                device_id_type=MESH,
            ))
        for copy in copies:
            copy.start()
        for copy in copies:
            copy.wait()
        total = col_slots[t, 0]
        for off in range(1, n_rows):
            total = total + col_slots[t, off]
        col_vec[...] = split_rows(ratio / total)

        def row_pass(where, block, index):
            mass = jnp.dot(col_vec[...], kern[:, where], preferred_element_type=F32)
            row_slots[t, me_cent, :, where] = jnp.sum(mass, axis=0, keepdims=True)

        blocks(rows, PASS_BLOCK, row_pass)
        copies = []
        for off in range(1, n_cent):
            copies.append(pltpu.make_async_remote_copy(
                src_ref=row_slots.at[t, me_cent],
                dst_ref=row_slots.at[t, me_cent],
                send_sem=row_send.at[t, off],
                recv_sem=row_recv.at[t, off],
                device_id={"cent": lax.rem(me_cent + off, n_cent)},
                device_id_type=MESH,
            ))
        for copy in copies:
            copy.start()
        for copy in copies:
            copy.wait()
        total = row_slots[t, 0]
        for other in range(1, n_cent):
            total = total + row_slots[t, other]
        scale = 1.0 / total
        if t < ITERS - 1:
            row_vec[...] = split_rows(scale)

            def col_pass(where, block, index):
                mass = lax.dot_general(
                    row_vec[...], kern[where, :], (((1,), (1,)), ((), ())),
                    preferred_element_type=F32,
                )
                col_slots[t + 1, 0, :, where] = jnp.sum(mass, axis=0, keepdims=True)

            blocks(n_local, PASS_BLOCK, col_pass)
        else:
            row_scale[...] = scale
            log_ref[...] = jnp.log(scale)

    out_block = min(CENT_BLOCK, n_local)
    steps = n_local // out_block

    def store(index, slot):
        at = pl.ds(pl.multiple_of(index * out_block, out_block), out_block)
        return pltpu.make_async_copy(out_buf.at[slot], sums_hbm.at[at], out_sem.at[slot])

    def weigh(index, carry):
        slot = lax.rem(index, 2)
        at = pl.ds(pl.multiple_of(index * out_block, out_block), out_block)

        @pl.when(index >= 2)
        def _():
            store(index - 2, slot).wait()

        total = jnp.zeros((out_block, width), F32)
        for b in range(rows // row_block):
            here = slice(b * row_block, (b + 1) * row_block)
            plan = (kern[at, here].astype(F32) * row_scale[:, here]).astype(BF16)
            total = total + jnp.dot(plan, unit[here, :], preferred_element_type=F32)
        out_buf[slot] = total
        store(index, slot).start()
        return carry

    lax.fori_loop(0, steps, weigh, 0)
    for index in range(max(steps - 2, 0), steps):
        store(index, index % 2).wait()


def balance(passages, centroids, n_rows, n_cent):
    rows, width = passages.shape
    n_local = centroids.shape[0]
    ratio = float(rows * n_rows) / float(n_local * n_cent)
    dma = pltpu.SemaphoreType.DMA
    return pl.pallas_call(
        functools.partial(sinkhorn_kernel, n_rows, n_cent, ratio),
        out_shape=(
            jax.ShapeDtypeStruct((n_local, width), F32),
            jax.ShapeDtypeStruct((1, rows), F32),
        ),
        in_specs=[pl.BlockSpec(memory_space=pl.ANY)] * 2,
        out_specs=(pl.BlockSpec(memory_space=pl.ANY), pl.BlockSpec(memory_space=pltpu.VMEM)),
        scratch_shapes=[
            pltpu.VMEM((n_local, rows), BF16),
            pltpu.VMEM((rows, width), BF16),
            pltpu.VMEM((n_local, width), BF16),
            pltpu.VMEM((2, min(CENT_BLOCK, n_local), width), F32),
            pltpu.VMEM((16, n_local), BF16),
            pltpu.VMEM((16, rows), BF16),
            pltpu.VMEM((1, rows), F32),
            pltpu.VMEM((ITERS, n_rows, 1, n_local), F32),
            pltpu.VMEM((ITERS, n_cent, 1, rows), F32),
            dma((5,)), dma((2,)),
            dma((ITERS, n_rows)), dma((ITERS, n_rows)),
            dma((ITERS, n_cent)), dma((ITERS, n_cent)),
        ],
        compiler_params=pltpu.CompilerParams(
            collective_id=0, has_side_effects=True, vmem_limit_bytes=60 * 1024 * 1024
        ),
        name="balance",
    )(passages, centroids)


def reduce_kernel(grid, streams, width, terms_hbm, out_hbm, total, *scratch):
    count = len(streams)
    landing = [scratch[3 * i:3 * i + 3] for i in range(count)]
    load_sem, own_sem, send_sem, recv_sem = scratch[3 * count:]
    me = lax.axis_index("rows")
    sizes = dict(zip("zyx", grid))
    strides = {"z": grid[1] * grid[2], "y": grid[2], "x": 1}
    at = {axis: lax.rem(lax.div(me, strides[axis]), sizes[axis]) for axis in "zyx"}

    def neighbour(axis, off):
        value = lax.rem(at[axis] + off, sizes[axis])
        return value, {"rows": me + (value - at[axis]) * strides[axis]}

    def load(i, p):
        order, start, rows, pieces = streams[i]
        where = pl.ds(start + p * rows, rows)
        return pltpu.make_async_copy(terms_hbm.at[where], total.at[where], load_sem.at[i, p])

    most = max(stream[3] for stream in streams)
    for p in range(most):
        for i in range(count):
            if p < streams[i][3]:
                load(i, p).start()

    barrier = pltpu.get_barrier_semaphore()
    for axis in "zyx":
        for off in range(1, sizes[axis]):
            pl.semaphore_signal(
                barrier, inc=1, device_id=neighbour(axis, off)[1], device_id_type=MESH
            )
    pl.semaphore_wait(barrier, sum(grid) - 3)

    def share(i, p, level, value):
        order, start, rows, pieces = streams[i]
        first, height = start + p * rows, rows
        for k in range(level + 1):
            height = height // sizes[order[k]]
            first = first + (value if k == level else at[order[k]]) * height
        return pl.ds(pl.multiple_of(first, 8), height)

    def reduces(i, p, level):
        axis = streams[i][0][level]
        copies = []
        for off in range(1, sizes[axis]):
            value, device = neighbour(axis, off)
            copies.append(pltpu.make_async_remote_copy(
                src_ref=total.at[share(i, p, level, value)],
                dst_ref=landing[i][level].at[p, off - 1],
                send_sem=send_sem.at[i, level, p, off - 1],
                recv_sem=recv_sem.at[i, level, p, off - 1],
                device_id=device, device_id_type=MESH,
            ))
        return copies

    def gathers(i, p, level):
        axis = streams[i][0][level]
        block = share(i, p, level, at[axis])
        source = total if level == 2 else out_hbm
        copies = []
        for off in range(1, sizes[axis]):
            copies.append(pltpu.make_async_remote_copy(
                src_ref=source.at[block], dst_ref=out_hbm.at[block],
                send_sem=send_sem.at[i, 5 - level, p, off - 1],
                recv_sem=recv_sem.at[i, 5 - level, p, off - 1],
                device_id=neighbour(axis, off)[1], device_id_type=MESH,
            ))
        return copies

    def own(i, p):
        block = share(i, p, 2, at[streams[i][0][2]])
        return pltpu.make_async_copy(total.at[block], out_hbm.at[block], own_sem.at[i, p])

    def accumulate(i, p, level):
        axis = streams[i][0][level]
        block = share(i, p, level, at[axis])
        height = block.size
        step = math.gcd(height, 32)

        def add(index, carry):
            here = pl.ds(pl.multiple_of(index * step, 8), step)
            there = pl.ds(pl.multiple_of(block.start + index * step, 8), step)
            value = total[there, :]
            for off in range(1, sizes[axis]):
                value = value + landing[i][level][p, off - 1, here, :]
            if level == 2:
                value = value * lax.rsqrt(jnp.mean(value * value, axis=-1, keepdims=True) + 1e-06)
            total[there, :] = value
            return carry

        lax.fori_loop(0, height // step, add, 0)

    def stage(i, p, number):
        if number == 0:
            load(i, p).wait()
        elif number <= 3:
            for copy in reduces(i, p, number - 1):
                copy.wait()
            accumulate(i, p, number - 1)
        else:
            for copy in gathers(i, p, 6 - number):
                copy.wait()
            if number == 4:
                own(i, p).wait()
        if number < 3:
            begin = reduces(i, p, number)
        elif number < 6:
            begin = gathers(i, p, 5 - number)
        else:
            begin = []
        for copy in begin:
            copy.start()
        if number == 3:
            own(i, p).start()

    for slot in range(most + 6):
        for number in range(7):
            for i in range(count):
                if 0 <= slot - number < streams[i][3]:
                    stage(i, slot - number, number)


def reduce_all(terms, n_rows):
    height, width = terms.shape
    grid = {16: (4, 2, 2), 32: (2, 4, 4)}.get(n_rows, (n_rows, 1, 1))
    half = height // 2
    pieces = max(1, min(PIECES, half // (8 * n_rows)))
    streams = (("xyz", 0, half // pieces, pieces), ("yxz", half, half // pieces, pieces))
    sizes = dict(zip("zyx", grid))
    landing = []
    for order, start, rows, count in streams:
        for axis in order:
            rows = rows // sizes[axis]
            landing.append(pltpu.VMEM((count, max(1, sizes[axis] - 1), rows, width), F32))
    dma = pltpu.SemaphoreType.DMA
    most = max(stream[3] for stream in streams)
    flags = dma((len(streams), 6, most, max(1, max(grid) - 1)))
    return pl.pallas_call(
        functools.partial(reduce_kernel, grid, streams, width),
        out_shape=jax.ShapeDtypeStruct((height, width), F32),
        in_specs=[pl.BlockSpec(memory_space=pl.ANY)],
        out_specs=pl.BlockSpec(memory_space=pl.ANY),
        scratch_shapes=[
            pltpu.VMEM((height, width), F32),
            *landing,
            dma((len(streams), most)), dma((len(streams), most)), flags, flags,
        ],
        compiler_params=pltpu.CompilerParams(
            collective_id=1, has_side_effects=True, vmem_limit_bytes=48 * 1024 * 1024
        ),
        name="reduce_all",
    )(terms)


def shards(n_rows, n_cent, passages, centroids):
    terms, logs = balance(passages, centroids, n_rows, n_cent)
    return (reduce_all(terms, n_rows), logs.reshape(-1))


def solution(mesh):
    placed = (P("rows", None), P("cent", None))
    return jax.shard_map(
        functools.partial(shards, mesh.shape["rows"], mesh.shape["cent"]),
        mesh=mesh, in_specs=placed, out_specs=(P("cent", None), P("rows")), check_vma=False,
    )
```

```python
import functools
import math

import jax
import jax.numpy as jnp
from jax import lax
from jax.experimental import pallas as pl
from jax.experimental.pallas import tpu as pltpu
from jax.sharding import PartitionSpec as P

ITERS = 3
MESH = pl.DeviceIdType.MESH
F32 = jnp.float32
BF16 = jnp.bfloat16
CENT_BLOCK = 256
ROW_BLOCK = 1024
PASS_BLOCK = 512
SHARES = (("xyz", 2, 8), ("yxz", 2, 8))


def unit_scale(values):
    full = values.astype(F32)
    return full * lax.rsqrt(jnp.mean(full * full, axis=-1, keepdims=True) + 1e-06)


def split_rows(vector):
    high = vector.astype(BF16).astype(F32)
    low = vector - high
    which = lax.broadcasted_iota(jnp.int32, (16, vector.shape[1]), 0)
    return jnp.where(which == 0, high, jnp.where(which == 1, low, 0.0)).astype(BF16)


def blocks(size, block, body):
    block = min(size, block)

    def step(index, carry):
        body(pl.ds(pl.multiple_of(index * block, block), block), block, index)
        return carry

    lax.fori_loop(0, size // block, step, 0)


def sinkhorn_kernel(
    n_rows, n_cent, ratio,
    rows_hbm, cents_hbm, sums_hbm, log_ref,
    kern, unit, cents, out_buf, col_vec, row_vec, row_scale,
    col_slots, row_slots, in_sem, out_sem, col_send, col_recv, row_send, row_recv,
):
    rows, width = unit.shape
    n_local = cents.shape[0]
    me_row = lax.axis_index("rows")
    me_cent = lax.axis_index("cent")
    part = rows // 4
    loads = [
        pltpu.make_async_copy(
            rows_hbm.at[pl.ds(q * part, part)], unit.at[pl.ds(q * part, part)], in_sem.at[q]
        )
        for q in range(4)
    ]
    loads.append(pltpu.make_async_copy(cents_hbm, cents, in_sem.at[4]))
    for load in loads:
        load.start()

    barrier = pltpu.get_barrier_semaphore()
    for off in range(1, n_rows):
        pl.semaphore_signal(
            barrier, inc=1, device_id={"rows": lax.rem(me_row + off, n_rows)}, device_id_type=MESH
        )
    for off in range(1, n_cent):
        pl.semaphore_signal(
            barrier, inc=1, device_id={"cent": lax.rem(me_cent + off, n_cent)}, device_id_type=MESH
        )

    for q in range(4):
        loads[q].wait()

        def normalize(where, block, index, q=q):
            at = pl.ds(pl.multiple_of(q * part + index * block, block), block)
            unit[at, :] = unit_scale(unit[at, :]).astype(BF16)

        blocks(part, 256, normalize)
    loads[4].wait()

    slope = 20.0 * math.log2(math.e) / width
    offset = 20.0 * math.log2(math.e)
    row_block = min(rows, ROW_BLOCK)

    def make_kernel(where, block, index):
        unit_cents = unit_scale(cents[where, :]).astype(BF16)
        acc = jnp.zeros((block, 128), F32)
        for b in range(rows // row_block):
            here = slice(b * row_block, (b + 1) * row_block)
            dot = lax.dot_general(
                unit_cents, unit[here, :], (((1,), (1,)), ((), ())), preferred_element_type=F32
            )
            value = jnp.exp2(dot * slope - offset)
            kern[where, here] = value.astype(BF16)
            for lane in range(row_block // 128):
                acc = acc + value[:, lane * 128:(lane + 1) * 128]
        col_slots[0, 0, :, where] = jnp.sum(acc.T, axis=0, keepdims=True)

    blocks(n_local, CENT_BLOCK, make_kernel)
    pl.semaphore_wait(barrier, n_rows - 1 + n_cent - 1)

    for t in range(ITERS):
        copies = []
        for off in range(1, n_rows):
            copies.append(pltpu.make_async_remote_copy(
                src_ref=col_slots.at[t, 0],
                dst_ref=col_slots.at[t, off],
                send_sem=col_send.at[t, off],
                recv_sem=col_recv.at[t, off],
                device_id={"rows": lax.rem(me_row + off, n_rows)},
                device_id_type=MESH,
            ))
        for copy in copies:
            copy.start()
        for copy in copies:
            copy.wait()
        total = col_slots[t, 0]
        for off in range(1, n_rows):
            total = total + col_slots[t, off]
        col_vec[...] = split_rows(ratio / total)

        def row_pass(where, block, index):
            mass = jnp.dot(col_vec[...], kern[:, where], preferred_element_type=F32)
            row_slots[t, me_cent, :, where] = jnp.sum(mass, axis=0, keepdims=True)

        blocks(rows, PASS_BLOCK, row_pass)
        copies = []
        for off in range(1, n_cent):
            copies.append(pltpu.make_async_remote_copy(
                src_ref=row_slots.at[t, me_cent],
                dst_ref=row_slots.at[t, me_cent],
                send_sem=row_send.at[t, off],
                recv_sem=row_recv.at[t, off],
                device_id={"cent": lax.rem(me_cent + off, n_cent)},
                device_id_type=MESH,
            ))
        for copy in copies:
            copy.start()
        for copy in copies:
            copy.wait()
        total = row_slots[t, 0]
        for other in range(1, n_cent):
            total = total + row_slots[t, other]
        scale = 1.0 / total
        if t < ITERS - 1:
            row_vec[...] = split_rows(scale)

            def col_pass(where, block, index):
                mass = lax.dot_general(
                    row_vec[...], kern[where, :], (((1,), (1,)), ((), ())),
                    preferred_element_type=F32,
                )
                col_slots[t + 1, 0, :, where] = jnp.sum(mass, axis=0, keepdims=True)

            blocks(n_local, PASS_BLOCK, col_pass)
        else:
            row_scale[...] = scale
            log_ref[...] = jnp.log(scale)

    out_block = min(CENT_BLOCK, n_local)
    steps = n_local // out_block

    def store(index, slot):
        at = pl.ds(pl.multiple_of(index * out_block, out_block), out_block)
        return pltpu.make_async_copy(out_buf.at[slot], sums_hbm.at[at], out_sem.at[slot])

    def weigh(index, carry):
        slot = lax.rem(index, 2)
        at = pl.ds(pl.multiple_of(index * out_block, out_block), out_block)

        @pl.when(index >= 2)
        def _():
            store(index - 2, slot).wait()

        total = jnp.zeros((out_block, width), F32)
        for b in range(rows // row_block):
            here = slice(b * row_block, (b + 1) * row_block)
            plan = (kern[at, here].astype(F32) * row_scale[:, here]).astype(BF16)
            total = total + jnp.dot(plan, unit[here, :], preferred_element_type=F32)
        out_buf[slot] = total
        store(index, slot).start()
        return carry

    lax.fori_loop(0, steps, weigh, 0)
    for index in range(max(steps - 2, 0), steps):
        store(index, index % 2).wait()


def balance(passages, centroids, n_rows, n_cent):
    rows, width = passages.shape
    n_local = centroids.shape[0]
    ratio = float(rows * n_rows) / float(n_local * n_cent)
    dma = pltpu.SemaphoreType.DMA
    return pl.pallas_call(
        functools.partial(sinkhorn_kernel, n_rows, n_cent, ratio),
        out_shape=(
            jax.ShapeDtypeStruct((n_local, width), F32),
            jax.ShapeDtypeStruct((1, rows), F32),
        ),
        in_specs=[pl.BlockSpec(memory_space=pl.ANY)] * 2,
        out_specs=(pl.BlockSpec(memory_space=pl.ANY), pl.BlockSpec(memory_space=pltpu.VMEM)),
        scratch_shapes=[
            pltpu.VMEM((n_local, rows), BF16),
            pltpu.VMEM((rows, width), BF16),
            pltpu.VMEM((n_local, width), BF16),
            pltpu.VMEM((2, min(CENT_BLOCK, n_local), width), F32),
            pltpu.VMEM((16, n_local), BF16),
            pltpu.VMEM((16, rows), BF16),
            pltpu.VMEM((1, rows), F32),
            pltpu.VMEM((ITERS, n_rows, 1, n_local), F32),
            pltpu.VMEM((ITERS, n_cent, 1, rows), F32),
            dma((5,)), dma((2,)),
            dma((ITERS, n_rows)), dma((ITERS, n_rows)),
            dma((ITERS, n_cent)), dma((ITERS, n_cent)),
        ],
        compiler_params=pltpu.CompilerParams(
            collective_id=0, has_side_effects=True, vmem_limit_bytes=60 * 1024 * 1024
        ),
        name="balance",
    )(passages, centroids)


def reduce_kernel(grid, streams, width, terms_hbm, out_hbm, total, *scratch):
    count = len(streams)
    landing = [scratch[3 * i:3 * i + 3] for i in range(count)]
    load_sem, own_sem, send_sem, recv_sem = scratch[3 * count:]
    me = lax.axis_index("rows")
    sizes = dict(zip("zyx", grid))
    strides = {"z": grid[1] * grid[2], "y": grid[2], "x": 1}
    at = {axis: lax.rem(lax.div(me, strides[axis]), sizes[axis]) for axis in "zyx"}

    def neighbour(axis, off):
        value = lax.rem(at[axis] + off, sizes[axis])
        return value, {"rows": me + (value - at[axis]) * strides[axis]}

    def load(i, p):
        order, start, rows, pieces = streams[i]
        where = pl.ds(start + p * rows, rows)
        return pltpu.make_async_copy(terms_hbm.at[where], total.at[where], load_sem.at[i, p])

    most = max(stream[3] for stream in streams)
    for p in range(most):
        for i in range(count):
            if p < streams[i][3]:
                load(i, p).start()

    barrier = pltpu.get_barrier_semaphore()
    for axis in "zyx":
        for off in range(1, sizes[axis]):
            pl.semaphore_signal(
                barrier, inc=1, device_id=neighbour(axis, off)[1], device_id_type=MESH
            )
    pl.semaphore_wait(barrier, sum(grid) - 3)

    def share(i, p, level, value):
        order, start, rows, pieces = streams[i]
        first, height = start + p * rows, rows
        for k in range(level + 1):
            height = height // sizes[order[k]]
            first = first + (value if k == level else at[order[k]]) * height
        return pl.ds(pl.multiple_of(first, 8), height)

    def reduces(i, p, level):
        axis = streams[i][0][level]
        copies = []
        for off in range(1, sizes[axis]):
            value, device = neighbour(axis, off)
            copies.append(pltpu.make_async_remote_copy(
                src_ref=total.at[share(i, p, level, value)],
                dst_ref=landing[i][level].at[p, off - 1],
                send_sem=send_sem.at[i, level, p, off - 1],
                recv_sem=recv_sem.at[i, level, p, off - 1],
                device_id=device, device_id_type=MESH,
            ))
        return copies

    def gathers(i, p, level):
        axis = streams[i][0][level]
        block = share(i, p, level, at[axis])
        source = total if level == 2 else out_hbm
        copies = []
        for off in range(1, sizes[axis]):
            copies.append(pltpu.make_async_remote_copy(
                src_ref=source.at[block], dst_ref=out_hbm.at[block],
                send_sem=send_sem.at[i, 5 - level, p, off - 1],
                recv_sem=recv_sem.at[i, 5 - level, p, off - 1],
                device_id=neighbour(axis, off)[1], device_id_type=MESH,
            ))
        return copies

    def own(i, p):
        block = share(i, p, 2, at[streams[i][0][2]])
        return pltpu.make_async_copy(total.at[block], out_hbm.at[block], own_sem.at[i, p])

    def accumulate(i, p, level):
        axis = streams[i][0][level]
        block = share(i, p, level, at[axis])
        height = block.size
        step = math.gcd(height, 32)

        def add(index, carry):
            here = pl.ds(pl.multiple_of(index * step, 8), step)
            there = pl.ds(pl.multiple_of(block.start + index * step, 8), step)
            value = total[there, :]
            for off in range(1, sizes[axis]):
                value = value + landing[i][level][p, off - 1, here, :]
            if level == 2:
                value = value * lax.rsqrt(jnp.mean(value * value, axis=-1, keepdims=True) + 1e-06)
            total[there, :] = value
            return carry

        lax.fori_loop(0, height // step, add, 0)

    def stage(i, p, number):
        if number == 0:
            load(i, p).wait()
        elif number <= 3:
            for copy in reduces(i, p, number - 1):
                copy.wait()
            accumulate(i, p, number - 1)
        else:
            for copy in gathers(i, p, 6 - number):
                copy.wait()
            if number == 4:
                own(i, p).wait()
        if number < 3:
            begin = reduces(i, p, number)
        elif number < 6:
            begin = gathers(i, p, 5 - number)
        else:
            begin = []
        for copy in begin:
            copy.start()
        if number == 3:
            own(i, p).start()

    for slot in range(most + 6):
        for number in range(7):
            for i in range(count):
                if 0 <= slot - number < streams[i][3]:
                    stage(i, slot - number, number)


def reduce_all(terms, n_rows, shares=SHARES):
    height, width = terms.shape
    grid = {16: (4, 2, 2), 32: (2, 4, 4)}.get(n_rows, (n_rows, 1, 1))
    if height * 2 // 32 % (8 * n_rows):
        shares = (("xyz", 1, 1), ("yxz", 1, 1))
    unit = height // sum(rows * pieces for order, rows, pieces in shares)
    streams, start = [], 0
    for order, rows, pieces in shares:
        streams.append((order, start, rows * unit, pieces))
        start += rows * unit * pieces
    sizes = dict(zip("zyx", grid))
    landing = []
    for order, start, rows, count in streams:
        for axis in order:
            rows = rows // sizes[axis]
            landing.append(pltpu.VMEM((count, max(1, sizes[axis] - 1), rows, width), F32))
    dma = pltpu.SemaphoreType.DMA
    most = max(stream[3] for stream in streams)
    flags = dma((len(streams), 6, most, max(1, max(grid) - 1)))
    return pl.pallas_call(
        functools.partial(reduce_kernel, grid, streams, width),
        out_shape=jax.ShapeDtypeStruct((height, width), F32),
        in_specs=[pl.BlockSpec(memory_space=pl.ANY)],
        out_specs=pl.BlockSpec(memory_space=pl.ANY),
        scratch_shapes=[
            pltpu.VMEM((height, width), F32),
            *landing,
            dma((len(streams), most)), dma((len(streams), most)), flags, flags,
        ],
        compiler_params=pltpu.CompilerParams(
            collective_id=1, has_side_effects=True, vmem_limit_bytes=48 * 1024 * 1024
        ),
        name="reduce_all",
    )(terms)


def shards(n_rows, n_cent, passages, centroids):
    terms, logs = balance(passages, centroids, n_rows, n_cent)
    return (reduce_all(terms, n_rows), logs.reshape(-1))


def solution(mesh):
    placed = (P("rows", None), P("cent", None))
    return jax.shard_map(
        functools.partial(shards, mesh.shape["rows"], mesh.shape["cent"]),
        mesh=mesh, in_specs=placed, out_specs=(P("cent", None), P("rows")), check_vma=False,
    )
```
